512 devices in a mesh: ctx: 32 (over y, z_lo, core), tp: 16 (over x, z_hi).
Axes of the slice: x: 4, y: 8, z: 8 (z_hi: 4, z_lo: 2; z = z_hi * 2 + z_lo), core: 2. Of those that a mesh axis runs over, the one named last changes fastest.
Arguments:
- quant_codes: bfloat16 [3, 4096, 8192], P(None, 'tp', 'ctx'), may hold values from -127 to 127
- block_scales: bfloat16 [3, 4096, 64], P(None, 'tp', 'ctx'), may hold values from 0.0029907227 to 0.029907227
- conv_taps: float32 [3, 4096, 3], P(None, 'tp'), may hold values from -3 to 3
- decay_rates: float32 [4096, 16], P('tp'), may hold values from 0.00012207031 to 0.05
- residues: float32 [4096, 16], P('tp'), may hold values from -2 to 2
- skip_gain: float32 [4096], P('tp'), may hold values from -4 to 4
- out_weight: bfloat16 [4096, 4096], P('tp'), may hold values from -0.125 to 0.125
Outputs:
- block_output: bfloat16 [4096, 8192], P('tp', 'ctx')
The draws below stay inside these ranges and needn't reach their ends.
All inputs are finite; a program needn't handle non-finite values.
Results may differ from the reference program's by a relative error of at most 0.015.
Values may be sent and summed in bfloat16 or wider, within the bound.
A program may use at most 64 MiB of HBM per device.

```python
import math
import jax
import jax.numpy as jnp
from jax import lax

DOUT = 4096
KS = 3
ORDER = 16
QB = 128
SEQ = 8192
CHANNELS = 4096


def raised(values, key, source, target, blocks, factor):
    owner, partner = [(jnp.arange(values.shape[axis_at]) // (values.shape[axis_at] // blocks)).reshape([-1 if axis == axis_at else 1 for axis in range(values.ndim)]) for axis_at in (source, target)]
    chosen = jax.random.permutation(key, blocks)[partner]
    strong = (owner == chosen) | (owner == (partner + blocks // 2) % blocks)
    return jnp.where(strong, factor * values, values)


def block_levels(key, dims, shards, least, top_value):
    def one(axis_at, shards_of):
        heights = jax.random.uniform(jax.random.fold_in(jax.random.fold_in(key, 6), axis_at), (shards_of,), jnp.float32, least / len(shards), top_value / len(shards))
        return jnp.repeat(jnp.exp(heights), dims[axis_at] // shards_of).reshape((-1,) + (1,) * (len(dims) - axis_at - 1))

    level = one(*shards[0])
    for cut in shards[1:]:
        level = level * one(*cut)
    return level


def scatter_about(own_key, shape, spread, bound, cuts=(), kind=jnp.bfloat16):
    array = jax.random.normal(own_key, shape, jnp.float32) * spread
    if len(cuts) > 0:
        array = block_levels(own_key, shape, cuts, -0.22, 0.18) * array
    return jnp.clip(array, min=-bound, max=bound).astype(kind)


def gaussian_with(own_key, extent, deviation, most, pieces, heavy, kind=jnp.bfloat16):
    values = deviation * jax.random.normal(own_key, extent, jnp.float32)
    if pieces:
        values = values * block_levels(own_key, extent, pieces, -0.22, 0.18)
    return jnp.clip(raised(values, jax.random.fold_in(own_key, 3), *heavy), -most, most).astype(kind)


def setup_inputs(seed: int = 0) -> dict:
    key_of = jax.random.split(jax.random.key(seed), 8)
    return {
        "quant_codes": jnp.clip(jax.random.uniform(key_of[0], (3, CHANNELS, SEQ), jnp.float32, -127.0, 127.0) * block_levels(key_of[0], (3, CHANNELS, SEQ), ((1, 16), (2, 32)), -0.4, 0.0), -127.0, 127.0).astype(jnp.bfloat16),
        "block_scales": jnp.clip(jnp.exp(math.log(0.029907227) - 2.3025851 * jax.random.uniform(key_of[1], (3, CHANNELS, SEQ // QB), jnp.float32) ** block_levels(key_of[1], (3, CHANNELS, SEQ // QB), ((1, 16), (2, 32)), -0.2, 0.2)), 0.0029907227, 0.029907227).astype(jnp.bfloat16),
        "conv_taps": scatter_about(key_of[2], (3, CHANNELS, KS), 0.6, 3.0, ((1, 16),), jnp.float32),
        "decay_rates": jnp.clip(jnp.exp(math.log(0.05) - 6.015181 * jax.random.uniform(key_of[3], (CHANNELS, ORDER), jnp.float32) ** block_levels(key_of[3], (CHANNELS, ORDER), ((0, 16),), -0.2, 0.2)), 0.00012207031, 0.05),
        "residues": scatter_about(key_of[4], (CHANNELS, ORDER), 0.35, 2.0, ((0, 16),), jnp.float32),
        "skip_gain": scatter_about(key_of[5], (CHANNELS,), 1.0, 4.0, ((0, 16),), jnp.float32),
        "out_weight": gaussian_with(key_of[6], (CHANNELS, DOUT), CHANNELS ** -0.5, 0.125, ((0, 16),), (0, 1, 16, 2.0)),
    }


def dequantize(codes, scales):
    block = codes.shape[-1] // scales.shape[-1]
    return codes.astype(jnp.float32) * jnp.repeat(scales.astype(jnp.float32), block, axis=-1)

def short_causal(values, taps):
    width = taps.shape[-1]
    length = values.shape[-1]
    padded = jnp.pad(values, ((0, 0), (0, 0), (width - 1, 0)))
    result = jnp.zeros(values.shape, jnp.float32)
    for offset in range(width):
        result = result + taps[:, :, offset:offset + 1] * padded[:, :, width - 1 - offset:width - 1 - offset + length]
    return result

def reference(quant_codes, block_scales, conv_taps, decay_rates, residues, skip_gain, out_weight):
    dequant = dequantize(quant_codes, block_scales)
    filtered = short_causal(dequant, conv_taps)
    product = (filtered[0] * filtered[2]).astype(jnp.bfloat16)
    gate_vals = filtered[1].astype(jnp.bfloat16)
    group = math.gcd(CHANNELS, 128)
    blocks = CHANNELS // group

    def one_block(inputs):
        signal, rates_here, weights_here, skip_here = inputs
        positions = jnp.arange(SEQ, dtype=jnp.float32)
        impulse = lax.optimization_barrier(jnp.sum((weights_here * jnp.sqrt(rates_here))[:, :, None] * jnp.exp(-rates_here[:, :, None] * positions), axis=1))
        spectrum = jnp.fft.rfft(signal, n=2 * SEQ, axis=-1) * jnp.fft.rfft(impulse, n=2 * SEQ, axis=-1)
        convolved = jnp.fft.irfft(spectrum, n=2 * SEQ, axis=-1)[:, :SEQ]
        return (convolved + skip_here[:, None] * signal).astype(jnp.bfloat16)
    long_conv = lax.map(one_block, (product.astype(jnp.float32).reshape(blocks, group, SEQ), decay_rates.reshape(blocks, group, ORDER), residues.reshape(blocks, group, ORDER), skip_gain.reshape(blocks, group)))
    long_conv = long_conv.reshape(CHANNELS, SEQ)
    gated = (gate_vals.astype(jnp.float32) * long_conv.astype(jnp.float32)).astype(jnp.bfloat16)
    summed = lax.dot_general(out_weight, gated, (((0,), (0,)), ((), ())), preferred_element_type=jnp.float32)
    return summed.astype(jnp.bfloat16)
```

```python
import functools

import jax
import jax.numpy as jnp
from jax import lax
from jax.experimental import pallas as pl
from jax.experimental.pallas import tpu as pltpu
from jax.sharding import PartitionSpec as P

MESH = pl.DeviceIdType.MESH
F32 = jnp.float32
BF16 = jnp.bfloat16

Y = 8
Q = 4
X = 4
Z = 4
C = 256
T = 256
O = 256
M = 16
SUB = 8
RUN = T // SUB
LANES = 128
PARTS = 4
ROWS = T // PARTS


def dot(a, b, dims=((1,), (0,))):
    return lax.dot_general(a, b, (dims, ((), ())), preferred_element_type=F32)


def place():
    row = lax.broadcasted_iota(jnp.int32, (T, T), 0)
    col = lax.broadcasted_iota(jnp.int32, (T, T), 1)
    return jnp.where((row % SUB) * RUN + row // SUB == col, 1.0, 0.0).astype(BF16)


def kernel(
    codes_h,
    scales_h,
    taps_h,
    rates_h,
    resid_h,
    skip_h,
    weight_h,
    out_ref,
    codes,
    scales,
    taps,
    rates,
    resid,
    skip,
    wbuf,
    deq,
    prod,
    gate,
    local,
    halo_out,
    halo_in,
    carry,
    decay,
    group_out,
    group_in,
    line_out,
    line_in,
    group_total_coef,
    group_before_coef,
    line_coef,
    entering,
    gown,
    gx,
    held,
    mine,
    opp_out,
    opp_in,
    side_out,
    side_in,
    load_sem,
    halo_sem,
    group_sem,
    line_sem,
    wx_sem,
    wcore_sem,
    wlow_sem,
    wpass_sem,
    gx_sem,
    gpass_sem,
    opp_sem,
    side_sem,
):
    ctx, tp = lax.axis_index("ctx"), lax.axis_index("tp")
    y, q = ctx // Q, ctx % Q
    x, z = tp // Z, tp % Z

    def at_ctx(index):
        return {"ctx": index, "tp": tp}

    def at_tp(index):
        return {"ctx": ctx, "tp": index}

    def group(d):
        return at_ctx(y * Q + q // 2 * 2 + (q + d) % 2 if d == 1 else y * Q + (q + 2) % 4 if d == 2 else y * Q + 3 - q)

    def line(d):
        return at_ctx((y + d) % Y * Q + q)

    def along_x(d):
        return at_tp((x + d) % X * Z + z)

    def along_z(d):
        return at_tp(x * Z + (z + d) % Z)

    def send(src, dst, sems, index, to):
        return pltpu.make_async_remote_copy(
            src_ref=src,
            dst_ref=dst,
            send_sem=sems.at[(0, *index)],
            recv_sem=sems.at[(1, *index)],
            device_id=to,
            device_id_type=MESH,
        )

    following, preceding = at_ctx((ctx + 1) % (Y * Q)), at_ctx((ctx + Y * Q - 1) % (Y * Q))

    barrier = pltpu.get_barrier_semaphore()
    partners = [following, preceding]
    partners += [group(d) for d in (1, 2, 3)]
    partners += [line(d) for d in range(1, Y)]
    partners += [along_x(d) for d in range(1, X)]
    partners += [along_z(d) for d in range(1, Z)]
    for partner in partners:
        pl.semaphore_signal(barrier, inc=1, device_id=partner, device_id_type=MESH)

    loads = [
        pltpu.make_async_copy(src, dst, load_sem.at[i])
        for i, (src, dst) in enumerate(
            [
                (codes_h, codes),
                (scales_h, scales),
                (taps_h, taps),
                (rates_h, rates),
                (resid_h, resid),
                (skip_h, skip),
            ]
        )
    ]
    own_weights = [
        pltpu.make_async_copy(
            weight_h.at[:, pl.ds(pl.multiple_of((x * Z + piece) * O, O), O)],
            wbuf.at[0, piece],
            load_sem.at[6 + piece],
        )
        for piece in range(Z)
    ]
    for load in loads + own_weights:
        load.start()
    for load in loads:
        load.wait()

    order = place()
    run_of = lax.broadcasted_iota(jnp.int32, (SUB, C), 0)
    scale_values = scales[...].astype(F32)
    for s in range(3):
        turned = dot(order, codes[s], ((1,), (1,)))
        scale = jnp.where(run_of < SUB // 2, scale_values[s, 0:1], scale_values[s, 1:2])
        values = (turned.reshape(RUN, SUB, C) * scale[None]).reshape(T, C)
        deq[s, 2 * SUB :, :] = values
        for back in (1, 2):
            last = values[T - back * SUB : T - (back - 1) * SUB]
            halo_out[2 * s + back - 1 : 2 * s + back, :] = last[SUB - 1 : SUB]
            before = jnp.where(run_of == 0, 0.0, pltpu.roll(last, 1, 0))
            deq[s, (2 - back) * SUB : (3 - back) * SUB, :] = before

    def filtered(s, start, rows):
        total = taps[s, 0:1, :] * deq[s, 2 * SUB + start : 2 * SUB + start + rows, :]
        for back in (1, 2):
            first = (2 - back) * SUB + start
            total = total + taps[s, back : back + 1, :] * deq[s, first : first + rows, :]
        return total

    def featurize(start, rows):
        product = (filtered(0, start, rows) * filtered(2, start, rows)).astype(BF16).astype(F32)
        gate[start : start + rows, :] = filtered(1, start, rows).astype(BF16).astype(F32)
        return product

    step = 32
    edge = 2 * SUB
    row16 = lax.broadcasted_iota(jnp.int32, (edge, C), 0)
    prod[0:edge, :] = jnp.where(row16 % SUB == 0, 0.0, featurize(0, edge))
    prod[edge : 2 * edge, :] = featurize(edge, edge)
    for start in range(step, T, step):
        prod[start : start + step, :] = featurize(start, step)

    pl.semaphore_wait(barrier, len(partners))

    halo = send(halo_out, halo_in, halo_sem, (), following)
    halo.start()
    over_x = []
    for d in (1, 3, 2):
        source = weight_h.at[:, pl.ds(pl.multiple_of(((x + d) % X * Z + q) * O, O), O)]
        over_x.append((d, send(source, wbuf.at[d, q], wx_sem, (d - 1,), along_x(d))))
    for _, copy in over_x:
        copy.start()

    a = rates[...]
    for m in range(M):
        decay[m] = jnp.broadcast_to(jnp.exp(-a[m : m + 1]), (SUB, C))
    for lanes in (slice(0, LANES), slice(LANES, C)):
        factor = decay[:, :, lanes]

        def state_step(j, state):
            return state * factor + prod[pl.ds(pl.multiple_of(j * SUB, SUB), SUB), lanes][None]

        carry[:, :, lanes] = lax.fori_loop(0, RUN, state_step, jnp.zeros((M, SUB, LANES), F32), unroll=4)
    for m in range(M):
        state = carry[m]
        rate = a[m : m + 1]
        for reach in (1, 2, 4):
            factor = jnp.where(run_of >= reach, jnp.exp(rate * (-float(reach * RUN))), 0.0)
            state = state + factor * pltpu.roll(state, reach, 0)
        group_out[m : m + 1, :] = state[SUB - 1 : SUB]
        carry[m] = jnp.where(run_of == 0, 0.0, pltpu.roll(state, 1, 0))

    def span(count):
        return jnp.exp(a * (-float(T) * count))

    for d in range(Q):
        source = q if d == 0 else (q // 2 * 2 + (q + 1) % 2 if d == 1 else (q + 2) % 4 if d == 2 else 3 - q)
        group_total_coef[d] = span((Q - 1 - source).astype(F32))
        reach = jnp.maximum(q - 1 - source, 0).astype(F32)
        group_before_coef[d] = jnp.where(source < q, span(reach), 0.0)
    for d in range(1, Y):
        line_coef[d - 1] = span((Q * (d - 1) + q).astype(F32))

    halo.wait()
    first = ctx == 0
    for s in range(3):
        for back in (1, 2):
            row = (2 - back) * SUB
            edge_row = halo_in[2 * s + back - 1 : 2 * s + back, :]
            deq[s, row : row + 1, :] = jnp.where(first, 0.0, edge_row)
    prod[0:edge, :] = featurize(0, edge)
    start0, start1 = prod[0:1, :], prod[SUB : SUB + 1, :]
    group_out[...] = (
        group_out[...] + jnp.exp(a * (1.0 - T)) * start0 + jnp.exp(a * (2.0 - T)) * start1
    )

    in_group = [send(group_out, group_in.at[d - 1], group_sem, (d - 1,), group(d)) for d in (1, 2, 3)]
    for copy in in_group:
        copy.start()

    mix = resid[...] * jnp.sqrt(a)
    for lanes in (slice(0, LANES), slice(LANES, C)):
        factor = decay[:, :, lanes]
        weight = jnp.stack([jnp.broadcast_to(mix[m : m + 1, lanes], (SUB, LANES)) for m in range(M)])

        def local_step(j, state):
            rows = pl.ds(pl.multiple_of(j * SUB, SUB), SUB)
            state = state * factor + prod[rows, lanes][None]
            local[rows, lanes] = jnp.sum(weight * state, axis=0)
            return state

        lax.fori_loop(0, RUN, local_step, jnp.zeros((M, SUB, LANES), F32), unroll=2)

    total = group_total_coef[0] * group_out[...]
    entry = jnp.zeros((M, C), F32)
    for d, copy in zip((1, 2, 3), in_group):
        copy.wait()
        total = total + group_total_coef[d] * group_in[d - 1]
        entry = entry + group_before_coef[d] * group_in[d - 1]
    line_out[...] = total
    entering[...] = entry

    in_line = [send(line_out, line_in.at[d - 1], line_sem, (d - 1,), line(d)) for d in range(1, Y)]
    for d, copy in zip(range(1, Y), in_line):
        pl.when(y + d < Y)(copy.start)

    to_core, to_low, passed = [], [], []
    for d, copy in over_x:
        copy.wait()
        piece = wbuf.at[d, q]
        to_core.append((d, send(piece, piece, wcore_sem, (d - 1,), group(1))))
        to_low.append((d, send(piece, piece, wlow_sem, (d - 1,), group(2))))
        to_low[-1][1].start()
        to_core[-1][1].start()

    for d, copy in zip(range(1, Y), in_line):
        @pl.when(y >= d)
        def _(d=d, copy=copy):
            copy.wait_recv()
            entering[...] = entering[...] + line_coef[d - 1] * line_in[d - 1]

        pl.when(y + d < Y)(copy.wait_send)

    edge_state = jnp.exp(a) * start0 + jnp.exp(a + a) * start1
    enters = entering[...]
    run_number = run_of.astype(F32)
    for m in range(M):
        own = jnp.where(run_of == 0, 0.0, edge_state[m : m + 1])
        reach = jnp.exp(a[m : m + 1] * (-float(RUN) * run_number))
        carry[m] = mix[m : m + 1] * (carry[m] + reach * (enters[m : m + 1] + own))

    gain = skip[...]
    for lanes in (slice(0, LANES), slice(LANES, C)):
        factor = decay[:, :, lanes]

        def join_step(j, state):
            rows = pl.ds(pl.multiple_of(j * 2 * SUB, 2 * SUB), 2 * SUB)
            state = state * factor
            upper = jnp.sum(state, axis=0)
            state = state * factor
            lower = jnp.sum(state, axis=0)
            long = jnp.concatenate([upper, lower], 0) + local[rows, lanes] + gain[:, lanes] * prod[rows, lanes]
            gown[rows, lanes] = (gate[rows, lanes] * long.astype(BF16).astype(F32)).astype(BF16)
            return state

        lax.fori_loop(0, RUN // 2, join_step, carry[:, :, lanes], unroll=2)

    def part(k):
        return pl.ds(k * ROWS, ROWS)

    gathers = []
    for k in range(PARTS):
        right = send(gown.at[part(k)], gx.at[0, part(k)], gx_sem, (0, k), along_x(1))
        left = send(gown.at[part(k)], gx.at[2, part(k)], gx_sem, (1, k), along_x(3))
        right.start()
        left.start()
        gathers.append((right, left))

    for d, copy in to_low:
        copy.wait()
        piece = wbuf.at[d, (q + 2) % 4]
        passed.append((d, send(piece, piece, wpass_sem, (d - 1,), group(1))))
        passed[-1][1].start()
    for d, copy in to_core:
        copy.wait()

    hands = []
    for k in range(PARTS):
        right, left = gathers[k]
        right.wait()
        left.wait()
        source, to = (0, 1) if k % 2 == 0 else (2, 3)
        hands.append(send(gx.at[source, part(k)], gx.at[1, part(k)], gpass_sem, (k,), along_x(to)))
        hands[-1].start()

    for load in own_weights:
        load.wait()
    for _, copy in passed:
        copy.wait()

    def block(k, shift):
        piece = (z + shift) % Z
        rows = part(k)
        result = dot(gown[rows, :], wbuf[0, piece])
        for d in (1, 3, 2):
            result = result + dot(gx[d - 1, rows, :], wbuf[d, piece])
        return result

    opposites, sides = [], []

    def finish(k):
        rows = part(k)
        opposites[k].wait()
        near = 1 if k % 2 == 0 else 3
        slot = 0 if near == 1 else 1
        side_out[slot, rows, :] = (held[rows, :] + opp_in[rows, :].astype(F32)).astype(BF16)
        copy = send(side_out.at[slot, rows], side_in.at[slot, rows], side_sem, (slot, k), along_z(near))
        copy.start()
        sides.append(copy)

    for k in range(PARTS):
        rows = part(k)
        hands[k].wait()
        near, far = (1, 3) if k % 2 == 0 else (3, 1)
        opp_out[rows, :] = block(k, 2).astype(BF16)
        copy = send(opp_out.at[rows], opp_in.at[rows], opp_sem, (k,), along_z(near))
        copy.start()
        opposites.append(copy)
        slot = 0 if far == 1 else 1
        side_out[slot, rows, :] = block(k, far).astype(BF16)
        copy = send(side_out.at[slot, rows], side_in.at[slot, rows], side_sem, (slot, k), along_z(far))
        copy.start()
        sides.append(copy)
        held[rows, :] = block(k, near)
        mine[rows, :] = block(k, 0)
        if k > 0:
            finish(k - 1)
    finish(PARTS - 1)
    for copy in sides:
        copy.wait()

    summed = mine[...] + side_in[0].astype(F32) + side_in[1].astype(F32)
    eye = jnp.where(
        lax.broadcasted_iota(jnp.int32, (O, O), 0) == lax.broadcasted_iota(jnp.int32, (O, O), 1), 1.0, 0.0
    ).astype(BF16)
    features = dot(eye, summed.astype(BF16), ((1,), (1,))).astype(BF16)
    out_ref[...] = dot(features, order).astype(BF16)


def on_device(quant_codes, block_scales, conv_taps, decay_rates, residues, skip_gain, out_weight):
    def vmem(shape, kind=F32):
        return pltpu.VMEM(shape, kind)

    dma = pltpu.SemaphoreType.DMA
    return pl.pallas_call(
        kernel,
        out_shape=jax.ShapeDtypeStruct((O, T), BF16),
        in_specs=[pl.BlockSpec(memory_space=pltpu.HBM)] * 7,
        out_specs=pl.BlockSpec(memory_space=pltpu.VMEM),
        scratch_shapes=[
            vmem((3, C, T), BF16),
            vmem((3, 2, C), BF16),
            vmem((3, 3, C)),
            vmem((M, C)),
            vmem((M, C)),
            vmem((1, C)),
            vmem((X, Z, C, O), BF16),
            vmem((3, T + 2 * SUB, C)),
            vmem((T, C)),
            vmem((T, C)),
            vmem((T, C)),
            vmem((SUB, C)),
            vmem((SUB, C)),
            vmem((M, SUB, C)),
            vmem((M, SUB, C)),
            vmem((M, C)),
            vmem((Q - 1, M, C)),
            vmem((M, C)),
            vmem((Y - 1, M, C)),
            vmem((Q, M, C)),
            vmem((Q, M, C)),
            vmem((Y - 1, M, C)),
            vmem((M, C)),
            vmem((T, C), BF16),
            vmem((X - 1, T, C), BF16),
            vmem((T, O)),
            vmem((T, O)),
            vmem((T, O), BF16),
            vmem((T, O), BF16),
            vmem((2, T, O), BF16),
            vmem((2, T, O), BF16),
            dma((6 + Z,)),
            dma((2,)),
            dma((2, Q - 1)),
            dma((2, Y - 1)),
            dma((2, X - 1)),
            dma((2, X - 1)),
            dma((2, X - 1)),
            dma((2, X - 1)),
            dma((2, 2, PARTS)),
            dma((2, PARTS)),
            dma((2, PARTS)),
            dma((2, 2, PARTS)),
        ],
        compiler_params=pltpu.CompilerParams(
            collective_id=0, has_side_effects=True, vmem_limit_bytes=60 * 1024 * 1024
        ),
        name="hyena",
    )(
        quant_codes,
        jnp.swapaxes(block_scales, 1, 2),
        jnp.swapaxes(conv_taps, 1, 2),
        decay_rates.T,
        residues.T,
        skip_gain.reshape(1, C),
        out_weight,
    )


def solution(mesh):
    return jax.shard_map(
        on_device,
        mesh=mesh,
        in_specs=(
            P(None, "tp", "ctx"),
            P(None, "tp", "ctx"),
            P(None, "tp", None),
            P("tp", None),
            P("tp", None),
            P("tp"),
            P("tp", None),
        ),
        out_specs=P("tp", "ctx"),
        check_vma=False,
    )
```

```python
import functools

import jax
import jax.numpy as jnp
from jax import lax
from jax.experimental import pallas as pl
from jax.experimental.pallas import tpu as pltpu
from jax.sharding import PartitionSpec as P

MESH = pl.DeviceIdType.MESH
F32 = jnp.float32
BF16 = jnp.bfloat16

Y = 8
Q = 4
X = 4
Z = 4
C = 256
T = 256
O = 256
M = 16
SUB = 8
RUN = T // SUB
LANES = 128
FIRST = M
LAST = FIRST + 4
EDGED = LAST + 4
PARTS = 4
ROWS = T // PARTS


def dot(a, b, dims=((1,), (0,))):
    return lax.dot_general(a, b, (dims, ((), ())), preferred_element_type=F32)


def place():
    row = lax.broadcasted_iota(jnp.int32, (T, T), 0)
    col = lax.broadcasted_iota(jnp.int32, (T, T), 1)
    return jnp.where((row % SUB) * RUN + row // SUB == col, 1.0, 0.0).astype(BF16)


def kernel(
    codes_h,
    scales_h,
    taps_h,
    rates_h,
    resid_h,
    skip_h,
    weight_h,
    out_ref,
    codes,
    scales,
    taps,
    rates,
    resid,
    skip,
    wbuf,
    deq,
    prod,
    gate,
    local,
    halo_out,
    halo_in,
    carry,
    decay,
    reach_table,
    group_in,
    line_in,
    edge_in,
    gown,
    gx,
    mine,
    sum_out,
    sum_in,
    load_sem,
    halo_sem,
    group_sem,
    edge_sem,
    line_sem,
    wx_sem,
    wcore_sem,
    wpair_sem,
    wpass_sem,
    gx_sem,
    sum_sem,
):
    ctx, tp = lax.axis_index("ctx"), lax.axis_index("tp")
    y, q = ctx // Q, ctx % Q
    x, z = tp // Z, tp % Z

    def at_ctx(index):
        return {"ctx": index, "tp": tp}

    def at_tp(index):
        return {"ctx": ctx, "tp": index}

    def group(d):
        return at_ctx(y * Q + q // 2 * 2 + (q + d) % 2 if d == 1 else y * Q + (q + 2) % 4 if d == 2 else y * Q + 3 - q)

    def line(d):
        return at_ctx((y + d) % Y * Q + q)

    def along_x(d):
        return at_tp((x + d) % X * Z + z)

    def along_z(d):
        return at_tp(x * Z + (z + d) % Z)

    def send(src, dst, sems, index, to):
        return pltpu.make_async_remote_copy(
            src_ref=src,
            dst_ref=dst,
            send_sem=sems.at[(0, *index)],
            recv_sem=sems.at[(1, *index)],
            device_id=to,
            device_id_type=MESH,
        )

    following, preceding = at_ctx((ctx + 1) % (Y * Q)), at_ctx((ctx + Y * Q - 1) % (Y * Q))

    codes_load = pltpu.make_async_copy(codes_h, codes, load_sem.at[0])
    small = [(scales_h, scales), (taps_h, taps), (rates_h, rates), (resid_h, resid), (skip_h, skip)]
    loads = [pltpu.make_async_copy(src, dst, load_sem.at[1 + i]) for i, (src, dst) in enumerate(small)]
    own_weights = [
        pltpu.make_async_copy(
            weight_h.at[:, pl.ds(pl.multiple_of((x * Z + piece) * O, O), O)],
            wbuf.at[0, piece],
            load_sem.at[6 + piece],
        )
        for piece in range(Z)
    ]
    for load in [codes_load] + loads:
        load.start()

    barrier = pltpu.get_barrier_semaphore()
    partners = [following, preceding]
    partners += [group(d) for d in (1, 2, 3)]
    partners += [line(d) for d in range(1, Y)]
    partners += [along_x(d) for d in range(1, X)]
    partners += [along_z(d) for d in range(1, Z)]
    for partner in partners:
        pl.semaphore_signal(barrier, inc=1, device_id=partner, device_id_type=MESH)
    group_before = (y + Y - 1) % Y * Q + Q - 1
    pl.semaphore_signal(barrier, inc=1, device_id=at_ctx(group_before), device_id_type=MESH)
    for load in own_weights:
        load.start()

    order = place()
    run_of = lax.broadcasted_iota(jnp.int32, (SUB, C), 0)
    for load in loads:
        load.wait()
    a = rates[...]
    fall = jnp.exp(-a)
    for m in range(M):
        decay[m] = jnp.broadcast_to(fall[m : m + 1], (SUB, C))
    fall_run = jnp.exp(a * (-float(RUN)))
    fall_own = jnp.exp(a * (-float(T)))
    from_first, from_second = jnp.exp(a * (1.0 - T)), jnp.exp(a * (2.0 - T))
    scale_values = scales[...].astype(F32)
    codes_load.wait()

    def dequantize(s):
        turned = dot(order, codes[s], ((1,), (1,)))
        scale = jnp.where(run_of < SUB // 2, scale_values[s, 0:1], scale_values[s, 1:2])
        values = (turned.reshape(RUN, SUB, C) * scale[None]).reshape(T, C)
        deq[s, 2 * SUB :, :] = values
        for back in (1, 2):
            last = values[T - back * SUB : T - (back - 1) * SUB]
            before = jnp.where(run_of == 0, 0.0, pltpu.roll(last, 1, 0))
            deq[s, (2 - back) * SUB : (3 - back) * SUB, :] = before

    def last_row(s, back):
        row = 2 * SUB + T - back * SUB + SUB - 1
        return deq[s, row : row + 1, :]

    def filtered(s, start, rows):
        total = taps[s, 0:1, :] * deq[s, 2 * SUB + start : 2 * SUB + start + rows, :]
        for back in (1, 2):
            first = (2 - back) * SUB + start
            total = total + taps[s, back : back + 1, :] * deq[s, first : first + rows, :]
        return total

    def products(start, rows):
        return (filtered(0, start, rows) * filtered(2, start, rows)).astype(BF16).astype(F32)

    dequantize(0)
    dequantize(2)
    step = 32
    edge = 2 * SUB
    row16 = lax.broadcasted_iota(jnp.int32, (edge, C), 0)
    prod[0:edge, :] = jnp.where(row16 % SUB == 0, 0.0, products(0, edge))
    prod[edge : 2 * edge, :] = products(edge, edge)
    for start in range(step, T, step):
        prod[start : start + step, :] = products(start, step)

    for lanes in (slice(0, LANES), slice(LANES, C)):
        factor = decay[:, :, lanes]

        def state_step(j, state):
            return state * factor + prod[pl.ds(pl.multiple_of(j * SUB, SUB), SUB), lanes][None]

        carry[:, :, lanes] = lax.fori_loop(0, RUN, state_step, jnp.zeros((M, SUB, LANES), F32), unroll=4)
    mine_in_group = group_in.at[q]
    for m in range(M):
        state = carry[m]
        power = fall_run[m : m + 1]
        for reach in (1, 2, 4):
            state = state + power * jnp.where(run_of >= reach, pltpu.roll(state, reach, 0), 0.0)
            power = power * power
        mine_in_group[m : m + 1, :] = state[SUB - 1 : SUB]
        carry[m] = jnp.where(run_of == 0, 0.0, pltpu.roll(state, 1, 0))
    for n, s in enumerate((0, 2)):
        for row in (0, 1):
            first = 2 * SUB + row * SUB
            mine_in_group[FIRST + 2 * n + row : FIRST + 2 * n + row + 1, :] = deq[s, first : first + 1, :]
            mine_in_group[LAST + 2 * n + row : LAST + 2 * n + row + 1, :] = last_row(s, 2 - row)

    pl.semaphore_wait(barrier, len(partners) + jnp.where(q == Q - 1, Q, 0))

    in_group = [send(mine_in_group, mine_in_group, group_sem, (d - 1,), group(d)) for d in (1, 2, 3)]
    to_next = [
        send(mine_in_group.at[FIRST:EDGED], edge_in, edge_sem, (j,), at_ctx((y + 1) % Y * Q + j)) for j in range(Q)
    ]
    for copy in in_group:
        copy.start()
    for copy in to_next:
        pl.when(q == Q - 1)(copy.start)

    quarters = (q, y % 2 * Q // 2 + q % 2)
    pair = (group(2), at_ctx((y // 2 * 2 + (y + 1) % 2) * Q + q))
    units = [(1, 0, 0, C), (3, 1, 0, C), (2, 0, 0, C // 2), (2, 1, C // 2, C // 2)]
    over_x = []
    for u, (d, way, start, rows) in enumerate(units):
        column = pl.multiple_of(((x + d) % X * Z + quarters[way]) * O, O)
        source = weight_h.at[pl.ds(start, rows), pl.ds(column, O)]
        over_x.append(send(source, wbuf.at[d, quarters[way], pl.ds(start, rows)], wx_sem, (u,), along_x(d)))
    for copy in over_x:
        copy.start()

    dequantize(1)
    for s in range(3):
        for back in (1, 2):
            halo_out[2 * s + back - 1 : 2 * s + back, :] = last_row(s, back)
    halo = send(halo_out, halo_in, halo_sem, (), following)
    halo.start()

    def first_terms(firsts, lasts):
        sides = []
        for n, s in enumerate((0, 2)):
            t0, t1, t2 = (taps[s, j : j + 1, :] for j in range(3))
            x0, x1 = firsts[2 * n : 2 * n + 1], firsts[2 * n + 1 : 2 * n + 2]
            b2, b1 = lasts[2 * n : 2 * n + 1], lasts[2 * n + 1 : 2 * n + 2]
            sides.append((t0 * x0 + t1 * b1 + t2 * b2, t0 * x1 + t1 * x0 + t2 * b1))
        p0, p1 = ((sides[0][i] * sides[1][i]).astype(BF16).astype(F32) for i in (0, 1))
        return from_first * p0 + from_second * p1

    for copy in in_group:
        copy.wait()
    for j in range(Q):
        pl.when(q == j)(to_next[j].wait_recv)
    total = jnp.zeros((M, C), F32)
    entry = jnp.zeros((M, C), F32)
    for source in range(Q):
        if source > 0:
            lasts = group_in[source - 1, LAST:EDGED, :]
        else:
            lasts = jnp.where(y == 0, 0.0, edge_in[LAST - FIRST :, :])
        state = group_in[source, 0:M, :] + first_terms(group_in[source, FIRST:LAST, :], lasts)
        entry = jnp.where(source < q, entry * fall_own + state, entry)
        total = total * fall_own + state
    line_in[y] = total

    mine_in_line = line_in.at[y]
    in_line = [send(mine_in_line, mine_in_line, line_sem, (d - 1,), line(d)) for d in range(1, Y)]
    for d, copy in zip(range(1, Y), in_line):
        pl.when(y + d < Y)(copy.start)

    halo.wait()
    first = ctx == 0
    for s in range(3):
        for back in (1, 2):
            row = (2 - back) * SUB
            edge_row = halo_in[2 * s + back - 1 : 2 * s + back, :]
            deq[s, row : row + 1, :] = jnp.where(first, 0.0, edge_row)
    prod[0:edge, :] = products(0, edge)
    for start in range(0, T, step):
        gate[start : start + step, :] = filtered(1, start, step).astype(BF16).astype(F32)
    mix = resid[...] * jnp.sqrt(a)
    for lanes in (slice(0, LANES), slice(LANES, C)):
        factor = decay[:, :, lanes]
        weight = jnp.stack([jnp.broadcast_to(mix[m : m + 1, lanes], (SUB, LANES)) for m in range(M)])

        def local_step(j, state):
            rows = pl.ds(pl.multiple_of(j * SUB, SUB), SUB)
            state = state * factor + prod[rows, lanes][None]
            local[rows, lanes] = jnp.sum(weight * state, axis=0)
            return state

        lax.fori_loop(0, RUN, local_step, jnp.zeros((M, SUB, LANES), F32), unroll=2)

    to_core, to_pair, passed = [], [], []
    for u, (d, way, start, rows) in enumerate(units):
        over_x[u].wait()
        piece = wbuf.at[d, quarters[way], pl.ds(start, rows)]
        to_pair.append(send(piece, piece, wpair_sem, (u,), pair[way]))
        to_core.append(send(piece, piece, wcore_sem, (u,), group(1)))
        to_pair[u].start()
        to_core[u].start()

    start0, start1 = prod[0:1, :], prod[SUB : SUB + 1, :]
    edge_state = jnp.exp(a) * start0 + jnp.exp(a + a) * start1
    run_number = run_of.astype(F32)
    for m in range(M):
        reaches = mix[m : m + 1] * jnp.exp(a[m : m + 1] * (-float(RUN) * run_number))
        reach_table[m] = reaches
        own = jnp.where(run_of == 0, 0.0, edge_state[m : m + 1])
        carry[m] = mix[m : m + 1] * carry[m] + reaches * own
    fall_group = jnp.exp(a * (-float(Q * T)))
    fall_entry = jnp.exp(a * (-float(T) * q.astype(F32)))

    for d, copy in zip(range(1, Y), in_line):
        pl.when(y >= d)(copy.wait_recv)
    enters = jnp.zeros((M, C), F32)
    for source in range(Y - 1):
        enters = jnp.where(source < y, enters * fall_group + line_in[source], enters)
    enters = enters * fall_entry + entry

    for m in range(M):
        carry[m] = carry[m] + reach_table[m] * enters[m : m + 1]

    gain = skip[...]
    for lanes in (slice(0, LANES), slice(LANES, C)):
        factor = decay[:, :, lanes]

        def join_step(j, state):
            rows = pl.ds(pl.multiple_of(j * 2 * SUB, 2 * SUB), 2 * SUB)
            state = state * factor
            upper = jnp.sum(state, axis=0)
            state = state * factor
            lower = jnp.sum(state, axis=0)
            long = jnp.concatenate([upper, lower], 0) + local[rows, lanes] + gain[:, lanes] * prod[rows, lanes]
            gown[rows, lanes] = (gate[rows, lanes] * long.astype(BF16).astype(F32)).astype(BF16)
            return state

        lax.fori_loop(0, RUN // 2, join_step, carry[:, :, lanes], unroll=2)

    for d, copy in zip(range(1, Y), in_line):
        pl.when(y + d < Y)(copy.wait_send)
    for copy in to_next:
        pl.when(q == Q - 1)(copy.wait_send)

    def part(k):
        return pl.ds(k * ROWS, ROWS)

    gathers = []
    for k in range(PARTS):
        gathers.append([send(gown.at[part(k)], gx.at[d - 1, part(k)], gx_sem, (d - 1, k), along_x(d)) for d in (2, 1, 3)])
        for copy in gathers[k]:
            copy.start()

    for u, (d, way, start, rows) in enumerate(units):
        to_pair[u].wait()
        piece = wbuf.at[d, (quarters[way] + 2) % Q, pl.ds(start, rows)]
        passed.append(send(piece, piece, wpass_sem, (u,), group(1)))
        passed[u].start()
    for load in own_weights:
        load.wait()
    for copy in to_core + passed:
        copy.wait()

    def block(k, piece):
        rows = part(k)
        result = dot(gown[rows, :], wbuf[0, piece])
        for d in (1, 3, 2):
            result = result + dot(gx[d - 1, rows, :], wbuf[d, piece])
        return result

    def message(k, to):
        slot = (to - z + Z - 1) % Z
        return send(sum_out.at[to, part(k)], sum_in.at[slot, part(k)], sum_sem, (slot, k), at_tp(x * Z + to))

    def work(k, to):
        rows = part(k)

        @pl.when(z == to)
        def _():
            mine[rows, :] = block(k, to)

        @pl.when(z != to)
        def _():
            sum_out[to, rows, :] = block(k, to).astype(BF16)
            message(k, to).start()

    for pieces in ((0, 2), (1, 3)):
        for k in range(PARTS):
            if pieces[0] == 0:
                for copy in gathers[k]:
                    copy.wait()
            for to in pieces:
                work(k, to)
    for k in range(PARTS):
        for to in range(Z):
            pl.when(z != to)(message(k, to).wait_send)
    for k in range(PARTS):
        rows = part(k)
        total = mine[rows, :]
        for shift in (1, 2, 3):
            here = send(sum_out.at[0, rows], sum_in.at[shift - 1, rows], sum_sem, (shift - 1, k), along_z(1))
            here.wait_recv()
            total = total + sum_in[shift - 1, rows, :].astype(F32)
        out_ref[rows, :] = total.astype(BF16)


def turn_kernel(rows_ref, out_ref):
    out_ref[...] = dot(rows_ref[...], place(), ((0,), (0,))).astype(BF16)


def on_device(quant_codes, block_scales, conv_taps, decay_rates, residues, skip_gain, out_weight):
    def vmem(shape, kind=F32):
        return pltpu.VMEM(shape, kind)

    dma = pltpu.SemaphoreType.DMA
    rows = pl.pallas_call(
        kernel,
        out_shape=jax.ShapeDtypeStruct((T, O), BF16),
        in_specs=[pl.BlockSpec(memory_space=pltpu.HBM)] * 7,
        out_specs=pl.BlockSpec(memory_space=pltpu.VMEM),
        scratch_shapes=[
            vmem((3, C, T), BF16),
            vmem((3, 2, C), BF16),
            vmem((3, 3, C)),
            vmem((M, C)),
            vmem((M, C)),
            vmem((1, C)),
            vmem((X, Z, C, O), BF16),
            vmem((3, T + 2 * SUB, C)),
            vmem((T, C)),
            vmem((T, C)),
            vmem((T, C)),
            vmem((SUB, C)),
            vmem((SUB, C)),
            vmem((M, SUB, C)),
            vmem((M, SUB, C)),
            vmem((M, SUB, C)),
            vmem((Q, EDGED, C)),
            vmem((Y, M, C)),
            vmem((EDGED - FIRST, C)),
            vmem((T, C), BF16),
            vmem((X - 1, T, C), BF16),
            vmem((T, O)),
            vmem((Z, T, O), BF16),
            vmem((Z - 1, T, O), BF16),
            dma((6 + Z,)),
            dma((2,)),
            dma((2, Q - 1)),
            dma((2, Q)),
            dma((2, Y - 1)),
            dma((2, 4)),
            dma((2, 4)),
            dma((2, 4)),
            dma((2, 4)),
            dma((2, X - 1, PARTS)),
            dma((2, Z - 1, PARTS)),
        ],
        compiler_params=pltpu.CompilerParams(
            collective_id=0, has_side_effects=True, vmem_limit_bytes=60 * 1024 * 1024
        ),
        name="hyena",
    )(
        quant_codes,
        jnp.swapaxes(block_scales, 1, 2),
        jnp.swapaxes(conv_taps, 1, 2),
        decay_rates.T,
        residues.T,
        skip_gain.reshape(1, C),
        out_weight,
    )
    return pl.pallas_call(
        turn_kernel,
        out_shape=jax.ShapeDtypeStruct((O, T), BF16),
        compiler_params=pltpu.CompilerParams(vmem_limit_bytes=60 * 1024 * 1024),
        name="turn",
    )(rows)


def solution(mesh):
    return jax.shard_map(
        on_device,
        mesh=mesh,
        in_specs=(
            P(None, "tp", "ctx"),
            P(None, "tp", "ctx"),
            P(None, "tp", None),
            P("tp", None),
            P("tp", None),
            P("tp"),
            P("tp", None),
        ),
        out_specs=P("tp", "ctx"),
        check_vma=False,
    )
```

```python
import functools

import jax
import jax.numpy as jnp
from jax import lax
from jax.experimental import pallas as pl
from jax.experimental.pallas import tpu as pltpu
from jax.sharding import PartitionSpec as P

MESH = pl.DeviceIdType.MESH
F32 = jnp.float32
BF16 = jnp.bfloat16

Y = 8
Q = 4
X = 4
Z = 4
C = 256
T = 256
O = 256
M = 16
SUB = 8
RUN = T // SUB
LANES = 128
FIRST = M
LAST = FIRST + 4
EDGED = LAST + 4
PARTS = 4
ROWS = T // PARTS


def dot(a, b, dims=((1,), (0,))):
    return lax.dot_general(a, b, (dims, ((), ())), preferred_element_type=F32)


def place():
    row = lax.broadcasted_iota(jnp.int32, (T, T), 0)
    col = lax.broadcasted_iota(jnp.int32, (T, T), 1)
    return jnp.where((row % SUB) * RUN + row // SUB == col, 1.0, 0.0).astype(BF16)


def kernel(
    codes_h,
    scales_h,
    taps_h,
    rates_h,
    resid_h,
    skip_h,
    weight_h,
    out_ref,
    codes,
    scales,
    taps,
    rates,
    resid,
    skip,
    wown,
    wfar,
    deq,
    prod,
    gate,
    local,
    halo_out,
    halo_in,
    carry,
    decay,
    reach_table,
    group_in,
    line_in,
    edge_in,
    gown,
    gx,
    mine,
    sum_out,
    sum_in,
    load_sem,
    halo_sem,
    group_sem,
    edge_sem,
    line_sem,
    wx_sem,
    wnear_sem,
    wcore_sem,
    gx_sem,
    sum_sem,
):
    ctx, tp = lax.axis_index("ctx"), lax.axis_index("tp")
    y, q = ctx // Q, ctx % Q
    x, z = tp // Z, tp % Z

    def at_ctx(index):
        return {"ctx": index, "tp": tp}

    def at_tp(index):
        return {"ctx": ctx, "tp": index}

    def group(d):
        return at_ctx(y * Q + q // 2 * 2 + (q + d) % 2 if d == 1 else y * Q + (q + 2) % 4 if d == 2 else y * Q + 3 - q)

    def line(d):
        return at_ctx((y + d) % Y * Q + q)

    def along_x(d):
        return at_tp((x + d) % X * Z + z)

    def along_z(d):
        return at_tp(x * Z + (z + d) % Z)

    def send(src, dst, sems, index, to):
        return pltpu.make_async_remote_copy(
            src_ref=src,
            dst_ref=dst,
            send_sem=sems.at[(0, *index)],
            recv_sem=sems.at[(1, *index)],
            device_id=to,
            device_id_type=MESH,
        )

    following, preceding = at_ctx((ctx + 1) % (Y * Q)), at_ctx((ctx + Y * Q - 1) % (Y * Q))

    codes_load = pltpu.make_async_copy(codes_h, codes, load_sem.at[0])
    small = [(scales_h, scales), (taps_h, taps), (rates_h, rates), (resid_h, resid), (skip_h, skip)]
    loads = [pltpu.make_async_copy(src, dst, load_sem.at[1 + i]) for i, (src, dst) in enumerate(small)]
    own_weights = [
        pltpu.make_async_copy(
            weight_h.at[:, pl.ds(pl.multiple_of((x * Z + piece) * O, O), O)],
            wown.at[piece],
            load_sem.at[6 + piece],
        )
        for piece in range(Z)
    ]
    for load in [codes_load] + loads:
        load.start()

    barrier = pltpu.get_barrier_semaphore()
    partners = [following, preceding]
    partners += [group(d) for d in (1, 2, 3)]
    partners += [line(d) for d in range(1, Y)]
    partners += [along_x(d) for d in range(1, X)]
    partners += [along_z(d) for d in range(1, Z)]
    for partner in partners:
        pl.semaphore_signal(barrier, inc=1, device_id=partner, device_id_type=MESH)
    group_before = (y + Y - 1) % Y * Q + Q - 1
    pl.semaphore_signal(barrier, inc=1, device_id=at_ctx(group_before), device_id_type=MESH)
    for load in own_weights:
        load.start()

    order = place()
    run_of = lax.broadcasted_iota(jnp.int32, (SUB, C), 0)
    for load in loads:
        load.wait()
    a = rates[...]
    fall = jnp.exp(-a)
    for m in range(M):
        decay[m] = jnp.broadcast_to(fall[m : m + 1], (SUB, C))
    fall_run = jnp.exp(a * (-float(RUN)))
    fall_own = jnp.exp(a * (-float(T)))
    from_first, from_second = jnp.exp(a * (1.0 - T)), jnp.exp(a * (2.0 - T))
    scale_values = scales[...].astype(F32)
    codes_load.wait()

    def dequantize(s):
        turned = dot(order, codes[s], ((1,), (1,)))
        scale = jnp.where(run_of < SUB // 2, scale_values[s, 0:1], scale_values[s, 1:2])
        values = (turned.reshape(RUN, SUB, C) * scale[None]).reshape(T, C)
        deq[s, 2 * SUB :, :] = values
        for back in (1, 2):
            last = values[T - back * SUB : T - (back - 1) * SUB]
            before = jnp.where(run_of == 0, 0.0, pltpu.roll(last, 1, 0))
            deq[s, (2 - back) * SUB : (3 - back) * SUB, :] = before

    def last_row(s, back):
        row = 2 * SUB + T - back * SUB + SUB - 1
        return deq[s, row : row + 1, :]

    def filtered(s, start, rows):
        total = taps[s, 0:1, :] * deq[s, 2 * SUB + start : 2 * SUB + start + rows, :]
        for back in (1, 2):
            first = (2 - back) * SUB + start
            total = total + taps[s, back : back + 1, :] * deq[s, first : first + rows, :]
        return total

    def products(start, rows):
        return (filtered(0, start, rows) * filtered(2, start, rows)).astype(BF16).astype(F32)

    dequantize(0)
    dequantize(2)
    step = 32
    edge = 2 * SUB
    row16 = lax.broadcasted_iota(jnp.int32, (edge, C), 0)
    prod[0:edge, :] = jnp.where(row16 % SUB == 0, 0.0, products(0, edge))
    prod[edge : 2 * edge, :] = products(edge, edge)
    for start in range(step, T, step):
        prod[start : start + step, :] = products(start, step)

    pl.semaphore_wait(barrier, len(partners) + jnp.where(q == Q - 1, Q, 0))

    colour, core = (y + q // 2 * 2) % Z, q % 2
    over_x = []
    for d in (1, 3, 2):
        column = pl.multiple_of(((x + d) % X * Z + colour) * O, O)
        source = weight_h.at[pl.ds(pl.multiple_of(core * (C // 2), C // 2), C // 2), pl.ds(column, O)]
        over_x.append(send(source, wfar.at[colour, core, d - 1], wx_sem, (d - 1,), along_x(d)))
    for copy in over_x:
        copy.start()

    for lanes in (slice(0, LANES), slice(LANES, C)):
        factor = decay[:, :, lanes]

        def state_step(j, state):
            return state * factor + prod[pl.ds(pl.multiple_of(j * SUB, SUB), SUB), lanes][None]

        carry[:, :, lanes] = lax.fori_loop(0, RUN, state_step, jnp.zeros((M, SUB, LANES), F32), unroll=4)
    mine_in_group = group_in.at[q]
    for m in range(M):
        state = carry[m]
        power = fall_run[m : m + 1]
        for reach in (1, 2, 4):
            state = state + power * jnp.where(run_of >= reach, pltpu.roll(state, reach, 0), 0.0)
            power = power * power
        mine_in_group[m : m + 1, :] = state[SUB - 1 : SUB]
        carry[m] = jnp.where(run_of == 0, 0.0, pltpu.roll(state, 1, 0))
    for n, s in enumerate((0, 2)):
        for row in (0, 1):
            first = 2 * SUB + row * SUB
            mine_in_group[FIRST + 2 * n + row : FIRST + 2 * n + row + 1, :] = deq[s, first : first + 1, :]
            mine_in_group[LAST + 2 * n + row : LAST + 2 * n + row + 1, :] = last_row(s, 2 - row)

    in_group = [send(mine_in_group, mine_in_group, group_sem, (d - 1,), group(d)) for d in (1, 2, 3)]
    to_next = [
        send(mine_in_group.at[FIRST:EDGED], edge_in, edge_sem, (j,), at_ctx((y + 1) % Y * Q + j)) for j in range(Q)
    ]
    for copy in in_group:
        copy.start()
    for copy in to_next:
        pl.when(q == Q - 1)(copy.start)

    dequantize(1)
    for s in range(3):
        for back in (1, 2):
            halo_out[2 * s + back - 1 : 2 * s + back, :] = last_row(s, back)
    halo = send(halo_out, halo_in, halo_sem, (), following)
    halo.start()

    def first_terms(firsts, lasts):
        sides = []
        for n, s in enumerate((0, 2)):
            t0, t1, t2 = (taps[s, j : j + 1, :] for j in range(3))
            x0, x1 = firsts[2 * n : 2 * n + 1], firsts[2 * n + 1 : 2 * n + 2]
            b2, b1 = lasts[2 * n : 2 * n + 1], lasts[2 * n + 1 : 2 * n + 2]
            sides.append((t0 * x0 + t1 * b1 + t2 * b2, t0 * x1 + t1 * x0 + t2 * b1))
        p0, p1 = ((sides[0][i] * sides[1][i]).astype(BF16).astype(F32) for i in (0, 1))
        return from_first * p0 + from_second * p1

    for copy in in_group:
        copy.wait()
    for j in range(Q):
        pl.when(q == j)(to_next[j].wait_recv)
    total = jnp.zeros((M, C), F32)
    entry = jnp.zeros((M, C), F32)
    for source in range(Q):
        if source > 0:
            lasts = group_in[source - 1, LAST:EDGED, :]
        else:
            lasts = jnp.where(y == 0, 0.0, edge_in[LAST - FIRST :, :])
        state = group_in[source, 0:M, :] + first_terms(group_in[source, FIRST:LAST, :], lasts)
        entry = jnp.where(source < q, entry * fall_own + state, entry)
        total = total * fall_own + state
    line_in[y] = total

    mine_in_line = line_in.at[y]
    in_line = [send(mine_in_line, mine_in_line, line_sem, (d - 1,), line(d)) for d in range(1, Y)]
    for d, copy in zip(range(1, Y), in_line):
        pl.when(y + d < Y)(copy.start)

    ways = ((group(2), 2), (line(1), Z - 1), (line(Y - 1), 1))
    spread, to_core = [], []
    for d, copy in zip((1, 3, 2), over_x):
        copy.wait()
        piece = wfar.at[colour, core, d - 1]
        for i, (to, _) in enumerate(ways):
            spread.append(send(piece, piece, wnear_sem, (i, d - 1), to))
        to_core.append(send(piece, piece, wcore_sem, (len(ways), d - 1), group(1)))
        for copy in spread[-len(ways) :] + to_core[-1:]:
            copy.start()

    halo.wait()
    first = ctx == 0
    for s in range(3):
        for back in (1, 2):
            row = (2 - back) * SUB
            edge_row = halo_in[2 * s + back - 1 : 2 * s + back, :]
            deq[s, row : row + 1, :] = jnp.where(first, 0.0, edge_row)
    prod[0:edge, :] = products(0, edge)
    for start in range(0, T, step):
        gate[start : start + step, :] = filtered(1, start, step).astype(BF16).astype(F32)
    mix = resid[...] * jnp.sqrt(a)
    for lanes in (slice(0, LANES), slice(LANES, C)):
        factor = decay[:, :, lanes]
        weight = jnp.stack([jnp.broadcast_to(mix[m : m + 1, lanes], (SUB, LANES)) for m in range(M)])

        def local_step(j, state):
            rows = pl.ds(pl.multiple_of(j * SUB, SUB), SUB)
            state = state * factor + prod[rows, lanes][None]
            local[rows, lanes] = jnp.sum(weight * state, axis=0)
            return state

        lax.fori_loop(0, RUN, local_step, jnp.zeros((M, SUB, LANES), F32), unroll=2)

    start0, start1 = prod[0:1, :], prod[SUB : SUB + 1, :]
    edge_state = jnp.exp(a) * start0 + jnp.exp(a + a) * start1
    run_number = run_of.astype(F32)
    for m in range(M):
        reaches = mix[m : m + 1] * jnp.exp(a[m : m + 1] * (-float(RUN) * run_number))
        reach_table[m] = reaches
        own = jnp.where(run_of == 0, 0.0, edge_state[m : m + 1])
        carry[m] = mix[m : m + 1] * carry[m] + reaches * own
    fall_group = jnp.exp(a * (-float(Q * T)))
    fall_entry = jnp.exp(a * (-float(T) * q.astype(F32)))

    for d, copy in zip(range(1, Y), in_line):
        pl.when(y >= d)(copy.wait_recv)
    enters = jnp.zeros((M, C), F32)
    for source in range(Y - 1):
        enters = jnp.where(source < y, enters * fall_group + line_in[source], enters)
    enters = enters * fall_entry + entry

    for m in range(M):
        carry[m] = carry[m] + reach_table[m] * enters[m : m + 1]

    gain = skip[...]
    for lanes in (slice(0, LANES), slice(LANES, C)):
        factor = decay[:, :, lanes]

        def join_step(j, state):
            rows = pl.ds(pl.multiple_of(j * 2 * SUB, 2 * SUB), 2 * SUB)
            state = state * factor
            upper = jnp.sum(state, axis=0)
            state = state * factor
            lower = jnp.sum(state, axis=0)
            long = jnp.concatenate([upper, lower], 0) + local[rows, lanes] + gain[:, lanes] * prod[rows, lanes]
            gown[rows, lanes] = (gate[rows, lanes] * long.astype(BF16).astype(F32)).astype(BF16)
            return state

        lax.fori_loop(0, RUN // 2, join_step, carry[:, :, lanes], unroll=2)

    for d, copy in zip(range(1, Y), in_line):
        pl.when(y + d < Y)(copy.wait_send)
    for copy in to_next:
        pl.when(q == Q - 1)(copy.wait_send)

    def part(k):
        return pl.ds(k * ROWS, ROWS)

    gathers = []
    for k in range(PARTS):
        gathers.append([send(gown.at[part(k)], gx.at[d - 1, part(k)], gx_sem, (d - 1, k), along_x(d)) for d in (2, 1, 3)])
        for copy in gathers[k]:
            copy.start()

    for n, d in enumerate((1, 3, 2)):
        for i, (_, ahead) in enumerate(ways):
            spread[n * len(ways) + i].wait()
            arrived = wfar.at[(colour + ahead) % Z, core, d - 1]
            to_core.append(send(arrived, arrived, wcore_sem, (i, d - 1), group(1)))
            to_core[-1].start()
    for load in own_weights:
        load.wait()
    for copy in to_core:
        copy.wait()

    def block(k, piece):
        rows = part(k)
        result = dot(gown[rows, :], wown[piece])
        for d in (1, 3, 2):
            weights = jnp.concatenate([wfar[piece, 0, d - 1], wfar[piece, 1, d - 1]], 0)
            result = result + dot(gx[d - 1, rows, :], weights)
        return result

    def message(k, to):
        slot = (to - z + Z - 1) % Z
        return send(sum_out.at[to, part(k)], sum_in.at[slot, part(k)], sum_sem, (slot, k), at_tp(x * Z + to))

    def work(k, to):
        rows = part(k)

        @pl.when(z == to)
        def _():
            mine[rows, :] = block(k, to)

        @pl.when(z != to)
        def _():
            sum_out[to, rows, :] = block(k, to).astype(BF16)
            message(k, to).start()

    for pieces in ((0, 2), (1, 3)):
        for k in range(PARTS):
            if pieces[0] == 0:
                for copy in gathers[k]:
                    copy.wait()
            for to in pieces:
                work(k, to)
    for k in range(PARTS):
        for to in range(Z):
            pl.when(z != to)(message(k, to).wait_send)
    for k in range(PARTS):
        rows = part(k)
        total = mine[rows, :]
        for shift in (1, 2, 3):
            here = send(sum_out.at[0, rows], sum_in.at[shift - 1, rows], sum_sem, (shift - 1, k), along_z(1))
            here.wait_recv()
            total = total + sum_in[shift - 1, rows, :].astype(F32)
        out_ref[rows, :] = total.astype(BF16)


def turn_kernel(rows_ref, out_ref):
    out_ref[...] = dot(rows_ref[...], place(), ((0,), (0,))).astype(BF16)


def on_device(quant_codes, block_scales, conv_taps, decay_rates, residues, skip_gain, out_weight):
    def vmem(shape, kind=F32):
        return pltpu.VMEM(shape, kind)

    dma = pltpu.SemaphoreType.DMA
    rows = pl.pallas_call(
        kernel,
        out_shape=jax.ShapeDtypeStruct((T, O), BF16),
        in_specs=[pl.BlockSpec(memory_space=pltpu.HBM)] * 7,
        out_specs=pl.BlockSpec(memory_space=pltpu.VMEM),
        scratch_shapes=[
            vmem((3, C, T), BF16),
            vmem((3, 2, C), BF16),
            vmem((3, 3, C)),
            vmem((M, C)),
            vmem((M, C)),
            vmem((1, C)),
            vmem((Z, C, O), BF16),
            vmem((Z, 2, X - 1, C // 2, O), BF16),
            vmem((3, T + 2 * SUB, C)),
            vmem((T, C)),
            vmem((T, C)),
            vmem((T, C)),
            vmem((SUB, C)),
            vmem((SUB, C)),
            vmem((M, SUB, C)),
            vmem((M, SUB, C)),
            vmem((M, SUB, C)),
            vmem((Q, EDGED, C)),
            vmem((Y, M, C)),
            vmem((EDGED - FIRST, C)),
            vmem((T, C), BF16),
            vmem((X - 1, T, C), BF16),
            vmem((T, O)),
            vmem((Z, T, O), BF16),
            vmem((Z - 1, T, O), BF16),
            dma((6 + Z,)),
            dma((2,)),
            dma((2, Q - 1)),
            dma((2, Q)),
            dma((2, Y - 1)),
            dma((2, X - 1)),
            dma((2, 3, X - 1)),
            dma((2, 4, X - 1)),
            dma((2, X - 1, PARTS)),
            dma((2, Z - 1, PARTS)),
        ],
        compiler_params=pltpu.CompilerParams(
            collective_id=0, has_side_effects=True, vmem_limit_bytes=60 * 1024 * 1024
        ),
        name="hyena",
    )(
        quant_codes,
        jnp.swapaxes(block_scales, 1, 2),
        jnp.swapaxes(conv_taps, 1, 2),
        decay_rates.T,
        residues.T,
        skip_gain.reshape(1, C),
        out_weight,
    )
    return pl.pallas_call(
        turn_kernel,
        out_shape=jax.ShapeDtypeStruct((O, T), BF16),
        compiler_params=pltpu.CompilerParams(vmem_limit_bytes=60 * 1024 * 1024),
        name="turn",
    )(rows)


def solution(mesh):
    return jax.shard_map(
        on_device,
        mesh=mesh,
        in_specs=(
            P(None, "tp", "ctx"),
            P(None, "tp", "ctx"),
            P(None, "tp", None),
            P("tp", None),
            P("tp", None),
            P("tp"),
            P("tp", None),
        ),
        out_specs=P("tp", "ctx"),
        check_vma=False,
    )
```

```python
import functools

import jax
import jax.numpy as jnp
from jax import lax
from jax.experimental import pallas as pl
from jax.experimental.pallas import tpu as pltpu
from jax.sharding import PartitionSpec as P

MESH = pl.DeviceIdType.MESH
F32 = jnp.float32
BF16 = jnp.bfloat16

Y = 8
Q = 4
X = 4
Z = 4
C = 256
T = 256
O = 256
M = 16
SUB = 8
RUN = T // SUB
LANES = 128
FIRST = M
LAST = FIRST + 4
EDGED = LAST + 4
PARTS = 4
ROWS = T // PARTS


def dot(a, b, dims=((1,), (0,))):
    return lax.dot_general(a, b, (dims, ((), ())), preferred_element_type=F32)


def place():
    row = lax.broadcasted_iota(jnp.int32, (T, T), 0)
    col = lax.broadcasted_iota(jnp.int32, (T, T), 1)
    return jnp.where((row % SUB) * RUN + row // SUB == col, 1.0, 0.0).astype(BF16)


def kernel(
    codes_h,
    scales_h,
    taps_h,
    rates_h,
    resid_h,
    skip_h,
    weight_h,
    out_ref,
    codes,
    scales,
    taps,
    rates,
    resid,
    skip,
    wown,
    wfar,
    deq,
    prod,
    gate,
    local,
    halo_out,
    halo_in,
    carry,
    decay,
    reach_table,
    group_in,
    line_in,
    edge_in,
    gown,
    gx,
    mine,
    sum_out,
    sum_in,
    load_sem,
    halo_sem,
    group_sem,
    edge_sem,
    line_sem,
    wx_sem,
    wnear_sem,
    wcore_sem,
    gx_sem,
    sum_sem,
):
    ctx, tp = lax.axis_index("ctx"), lax.axis_index("tp")
    y, q = ctx // Q, ctx % Q
    x, z = tp // Z, tp % Z

    def at_ctx(index):
        return {"ctx": index, "tp": tp}

    def at_tp(index):
        return {"ctx": ctx, "tp": index}

    def group(d):
        return at_ctx(y * Q + q // 2 * 2 + (q + d) % 2 if d == 1 else y * Q + (q + 2) % 4 if d == 2 else y * Q + 3 - q)

    def line(d):
        return at_ctx((y + d) % Y * Q + q)

    def along_x(d):
        return at_tp((x + d) % X * Z + z)

    def along_z(d):
        return at_tp(x * Z + (z + d) % Z)

    def send(src, dst, sems, index, to):
        return pltpu.make_async_remote_copy(
            src_ref=src,
            dst_ref=dst,
            send_sem=sems.at[(0, *index)],
            recv_sem=sems.at[(1, *index)],
            device_id=to,
            device_id_type=MESH,
        )

    following, preceding = at_ctx((ctx + 1) % (Y * Q)), at_ctx((ctx + Y * Q - 1) % (Y * Q))

    codes_load = pltpu.make_async_copy(codes_h, codes, load_sem.at[0])
    small = [(scales_h, scales), (taps_h, taps), (rates_h, rates), (resid_h, resid), (skip_h, skip)]
    loads = [pltpu.make_async_copy(src, dst, load_sem.at[1 + i]) for i, (src, dst) in enumerate(small)]
    own_weights = [
        pltpu.make_async_copy(
            weight_h.at[:, pl.ds(pl.multiple_of((x * Z + piece) * O, O), O)],
            wown.at[piece],
            load_sem.at[6 + piece],
        )
        for piece in range(Z)
    ]
    for load in [codes_load] + loads:
        load.start()

    barrier = pltpu.get_barrier_semaphore()
    partners = [following, preceding]
    partners += [group(d) for d in (1, 2, 3)]
    partners += [line(d) for d in range(1, Y)]
    partners += [along_x(d) for d in range(1, X)]
    partners += [along_z(d) for d in range(1, Z)]
    for partner in partners:
        pl.semaphore_signal(barrier, inc=1, device_id=partner, device_id_type=MESH)
    group_before = (y + Y - 1) % Y * Q + Q - 1
    pl.semaphore_signal(barrier, inc=1, device_id=at_ctx(group_before), device_id_type=MESH)
    for load in own_weights:
        load.start()

    order = place()
    run_of = lax.broadcasted_iota(jnp.int32, (SUB, C), 0)
    for load in loads:
        load.wait()
    a = rates[...]
    fall = jnp.exp(-a)
    for m in range(M):
        decay[m] = jnp.broadcast_to(fall[m : m + 1], (SUB, C))
    fall_run = jnp.exp(a * (-float(RUN)))
    fall_own = jnp.exp(a * (-float(T)))
    from_first, from_second = jnp.exp(a * (1.0 - T)), jnp.exp(a * (2.0 - T))
    scale_values = scales[...].astype(F32)
    codes_load.wait()

    def dequantize(s):
        turned = dot(order, codes[s], ((1,), (1,)))
        scale = jnp.where(run_of < SUB // 2, scale_values[s, 0:1], scale_values[s, 1:2])
        values = (turned.reshape(RUN, SUB, C) * scale[None]).reshape(T, C)
        deq[s, 2 * SUB :, :] = values
        for back in (1, 2):
            last = values[T - back * SUB : T - (back - 1) * SUB]
            before = jnp.where(run_of == 0, 0.0, pltpu.roll(last, 1, 0))
            deq[s, (2 - back) * SUB : (3 - back) * SUB, :] = before

    def last_row(s, back):
        row = 2 * SUB + T - back * SUB + SUB - 1
        return deq[s, row : row + 1, :]

    def filtered(s, start, rows):
        total = taps[s, 0:1, :] * deq[s, 2 * SUB + start : 2 * SUB + start + rows, :]
        for back in (1, 2):
            first = (2 - back) * SUB + start
            total = total + taps[s, back : back + 1, :] * deq[s, first : first + rows, :]
        return total

    def products(start, rows):
        return (filtered(0, start, rows) * filtered(2, start, rows)).astype(BF16).astype(F32)

    dequantize(0)
    dequantize(2)
    step = 32
    edge = 2 * SUB
    row16 = lax.broadcasted_iota(jnp.int32, (edge, C), 0)
    prod[0:edge, :] = jnp.where(row16 % SUB == 0, 0.0, products(0, edge))
    prod[edge : 2 * edge, :] = products(edge, edge)
    for start in range(step, T, step):
        prod[start : start + step, :] = products(start, step)

    pl.semaphore_wait(barrier, len(partners) + jnp.where(q == Q - 1, Q, 0))

    colour, core = (y + q // 2 * 2) % Z, q % 2
    over_x = []
    for d in (1, 3, 2):
        column = pl.multiple_of(((x + d) % X * Z + colour) * O, O)
        source = weight_h.at[pl.ds(pl.multiple_of(core * (C // 2), C // 2), C // 2), pl.ds(column, O)]
        over_x.append(send(source, wfar.at[colour, core, d - 1], wx_sem, (d - 1,), along_x(d)))

    for lanes in (slice(0, LANES), slice(LANES, C)):
        factor = decay[:, :, lanes]

        def state_step(j, state):
            return state * factor + prod[pl.ds(pl.multiple_of(j * SUB, SUB), SUB), lanes][None]

        carry[:, :, lanes] = lax.fori_loop(0, RUN, state_step, jnp.zeros((M, SUB, LANES), F32), unroll=4)
    mine_in_group = group_in.at[q]
    for m in range(M):
        state = carry[m]
        power = fall_run[m : m + 1]
        for reach in (1, 2, 4):
            state = state + power * jnp.where(run_of >= reach, pltpu.roll(state, reach, 0), 0.0)
            power = power * power
        mine_in_group[m : m + 1, :] = state[SUB - 1 : SUB]
        carry[m] = jnp.where(run_of == 0, 0.0, pltpu.roll(state, 1, 0))
    for n, s in enumerate((0, 2)):
        for row in (0, 1):
            first = 2 * SUB + row * SUB
            mine_in_group[FIRST + 2 * n + row : FIRST + 2 * n + row + 1, :] = deq[s, first : first + 1, :]
            mine_in_group[LAST + 2 * n + row : LAST + 2 * n + row + 1, :] = last_row(s, 2 - row)

    in_group = [send(mine_in_group, mine_in_group, group_sem, (d - 1,), group(d)) for d in (1, 2, 3)]
    to_next = [
        send(mine_in_group.at[FIRST:EDGED], edge_in, edge_sem, (j,), at_ctx((y + 1) % Y * Q + j)) for j in range(Q)
    ]
    for copy in in_group:
        copy.start()
    for copy in to_next:
        pl.when(q == Q - 1)(copy.start)

    for copy in over_x:
        copy.start()

    dequantize(1)
    for s in range(3):
        for back in (1, 2):
            halo_out[2 * s + back - 1 : 2 * s + back, :] = last_row(s, back)
    halo = send(halo_out, halo_in, halo_sem, (), following)
    halo.start()

    def first_terms(firsts, lasts):
        sides = []
        for n, s in enumerate((0, 2)):
            t0, t1, t2 = (taps[s, j : j + 1, :] for j in range(3))
            x0, x1 = firsts[2 * n : 2 * n + 1], firsts[2 * n + 1 : 2 * n + 2]
            b2, b1 = lasts[2 * n : 2 * n + 1], lasts[2 * n + 1 : 2 * n + 2]
            sides.append((t0 * x0 + t1 * b1 + t2 * b2, t0 * x1 + t1 * x0 + t2 * b1))
        p0, p1 = ((sides[0][i] * sides[1][i]).astype(BF16).astype(F32) for i in (0, 1))
        return from_first * p0 + from_second * p1

    for copy in in_group:
        copy.wait()
    for j in range(Q):
        pl.when(q == j)(to_next[j].wait_recv)
    total = jnp.zeros((M, C), F32)
    entry = jnp.zeros((M, C), F32)
    for source in range(Q):
        if source > 0:
            lasts = group_in[source - 1, LAST:EDGED, :]
        else:
            lasts = jnp.where(y == 0, 0.0, edge_in[LAST - FIRST :, :])
        state = group_in[source, 0:M, :] + first_terms(group_in[source, FIRST:LAST, :], lasts)
        entry = jnp.where(source < q, entry * fall_own + state, entry)
        total = total * fall_own + state
    line_in[y] = total

    mine_in_line = line_in.at[y]
    in_line = [send(mine_in_line, mine_in_line, line_sem, (d - 1,), line(d)) for d in range(1, Y)]
    for d in sorted(range(1, Y), key=lambda d: -min(d, Y - d)):
        pl.when(y + d < Y)(in_line[d - 1].start)

    ways = ((group(2), 2), (line(1), Z - 1), (line(Y - 1), 1))
    spread, to_core = [], []
    for d, copy in zip((1, 3, 2), over_x):
        copy.wait()
        piece = wfar.at[colour, core, d - 1]
        for i, (to, _) in enumerate(ways):
            spread.append(send(piece, piece, wnear_sem, (i, d - 1), to))
        to_core.append(send(piece, piece, wcore_sem, (len(ways), d - 1), group(1)))
        for copy in spread[-len(ways) :] + to_core[-1:]:
            copy.start()

    halo.wait()
    first = ctx == 0
    for s in range(3):
        for back in (1, 2):
            row = (2 - back) * SUB
            edge_row = halo_in[2 * s + back - 1 : 2 * s + back, :]
            deq[s, row : row + 1, :] = jnp.where(first, 0.0, edge_row)
    prod[0:edge, :] = products(0, edge)
    for start in range(0, T, step):
        gate[start : start + step, :] = filtered(1, start, step).astype(BF16).astype(F32)
    mix = resid[...] * jnp.sqrt(a)
    for lanes in (slice(0, LANES), slice(LANES, C)):
        factor = decay[:, :, lanes]
        weight = jnp.stack([jnp.broadcast_to(mix[m : m + 1, lanes], (SUB, LANES)) for m in range(M)])

        def local_step(j, state):
            rows = pl.ds(pl.multiple_of(j * SUB, SUB), SUB)
            state = state * factor + prod[rows, lanes][None]
            local[rows, lanes] = jnp.sum(weight * state, axis=0)
            return state

        lax.fori_loop(0, RUN, local_step, jnp.zeros((M, SUB, LANES), F32), unroll=2)

    start0, start1 = prod[0:1, :], prod[SUB : SUB + 1, :]
    edge_state = jnp.exp(a) * start0 + jnp.exp(a + a) * start1
    run_number = run_of.astype(F32)
    for m in range(M):
        reaches = mix[m : m + 1] * jnp.exp(a[m : m + 1] * (-float(RUN) * run_number))
        reach_table[m] = reaches
        own = jnp.where(run_of == 0, 0.0, edge_state[m : m + 1])
        carry[m] = mix[m : m + 1] * carry[m] + reaches * own
    fall_group = jnp.exp(a * (-float(Q * T)))
    fall_entry = jnp.exp(a * (-float(T) * q.astype(F32)))

    for d, copy in zip(range(1, Y), in_line):
        pl.when(y >= d)(copy.wait_recv)
    enters = jnp.zeros((M, C), F32)
    for source in range(Y - 1):
        enters = jnp.where(source < y, enters * fall_group + line_in[source], enters)
    enters = enters * fall_entry + entry

    for m in range(M):
        carry[m] = carry[m] + reach_table[m] * enters[m : m + 1]

    gain = skip[...]
    for lanes in (slice(0, LANES), slice(LANES, C)):
        factor = decay[:, :, lanes]

        def join_step(j, state):
            rows = pl.ds(pl.multiple_of(j * 2 * SUB, 2 * SUB), 2 * SUB)
            state = state * factor
            upper = jnp.sum(state, axis=0)
            state = state * factor
            lower = jnp.sum(state, axis=0)
            long = jnp.concatenate([upper, lower], 0) + local[rows, lanes] + gain[:, lanes] * prod[rows, lanes]
            gown[rows, lanes] = (gate[rows, lanes] * long.astype(BF16).astype(F32)).astype(BF16)
            return state

        lax.fori_loop(0, RUN // 2, join_step, carry[:, :, lanes], unroll=2)

    for d, copy in zip(range(1, Y), in_line):
        pl.when(y + d < Y)(copy.wait_send)
    for copy in to_next:
        pl.when(q == Q - 1)(copy.wait_send)

    def part(k):
        return pl.ds(k * ROWS, ROWS)

    gathers = []
    for k in range(PARTS):
        gathers.append([send(gown.at[part(k)], gx.at[d - 1, part(k)], gx_sem, (d - 1, k), along_x(d)) for d in (1, 3, 2)])
        for copy in gathers[k]:
            copy.start()

    for n, d in enumerate((1, 3, 2)):
        for i, (_, ahead) in enumerate(ways):
            spread[n * len(ways) + i].wait()
            arrived = wfar.at[(colour + ahead) % Z, core, d - 1]
            to_core.append(send(arrived, arrived, wcore_sem, (i, d - 1), group(1)))
            to_core[-1].start()
    for load in own_weights:
        load.wait()
    for copy in to_core:
        copy.wait()

    def block(k, piece):
        rows = part(k)
        result = dot(gown[rows, :], wown[piece])
        for d in (1, 3, 2):
            weights = jnp.concatenate([wfar[piece, 0, d - 1], wfar[piece, 1, d - 1]], 0)
            result = result + dot(gx[d - 1, rows, :], weights)
        return result

    def message(k, to):
        slot = (to - z + Z - 1) % Z
        return send(sum_out.at[to, part(k)], sum_in.at[slot, part(k)], sum_sem, (slot, k), at_tp(x * Z + to))

    def work(k, to):
        rows = part(k)

        @pl.when(z == to)
        def _():
            mine[rows, :] = block(k, to)

        @pl.when(z != to)
        def _():
            sum_out[to, rows, :] = block(k, to).astype(BF16)
            message(k, to).start()

    for pieces in ((0, 2), (1, 3)):
        for k in range(PARTS):
            if pieces[0] == 0:
                for copy in gathers[k]:
                    copy.wait()
            for to in pieces:
                work(k, to)
    for k in range(PARTS):
        for to in range(Z):
            pl.when(z != to)(message(k, to).wait_send)
    for k in range(PARTS):
        rows = part(k)
        total = mine[rows, :]
        for shift in (1, 2, 3):
            here = send(sum_out.at[0, rows], sum_in.at[shift - 1, rows], sum_sem, (shift - 1, k), along_z(1))
            here.wait_recv()
            total = total + sum_in[shift - 1, rows, :].astype(F32)
        out_ref[rows, :] = total.astype(BF16)


def turn_kernel(rows_ref, out_ref):
    out_ref[...] = dot(rows_ref[...], place(), ((0,), (0,))).astype(BF16)


def on_device(quant_codes, block_scales, conv_taps, decay_rates, residues, skip_gain, out_weight):
    def vmem(shape, kind=F32):
        return pltpu.VMEM(shape, kind)

    dma = pltpu.SemaphoreType.DMA
    rows = pl.pallas_call(
        kernel,
        out_shape=jax.ShapeDtypeStruct((T, O), BF16),
        in_specs=[pl.BlockSpec(memory_space=pltpu.HBM)] * 7,
        out_specs=pl.BlockSpec(memory_space=pltpu.VMEM),
        scratch_shapes=[
            vmem((3, C, T), BF16),
            vmem((3, 2, C), BF16),
            vmem((3, 3, C)),
            vmem((M, C)),
            vmem((M, C)),
            vmem((1, C)),
            vmem((Z, C, O), BF16),
            vmem((Z, 2, X - 1, C // 2, O), BF16),
            vmem((3, T + 2 * SUB, C)),
            vmem((T, C)),
            vmem((T, C)),
            vmem((T, C)),
            vmem((SUB, C)),
            vmem((SUB, C)),
            vmem((M, SUB, C)),
            vmem((M, SUB, C)),
            vmem((M, SUB, C)),
            vmem((Q, EDGED, C)),
            vmem((Y, M, C)),
            vmem((EDGED - FIRST, C)),
            vmem((T, C), BF16),
            vmem((X - 1, T, C), BF16),
            vmem((T, O)),
            vmem((Z, T, O), BF16),
            vmem((Z - 1, T, O), BF16),
            dma((6 + Z,)),
            dma((2,)),
            dma((2, Q - 1)),
            dma((2, Q)),
            dma((2, Y - 1)),
            dma((2, X - 1)),
            dma((2, 3, X - 1)),
            dma((2, 4, X - 1)),
            dma((2, X - 1, PARTS)),
            dma((2, Z - 1, PARTS)),
        ],
        compiler_params=pltpu.CompilerParams(
            collective_id=0, has_side_effects=True, vmem_limit_bytes=60 * 1024 * 1024
        ),
        name="hyena",
    )(
        quant_codes,
        jnp.swapaxes(block_scales, 1, 2),
        jnp.swapaxes(conv_taps, 1, 2),
        decay_rates.T,
        residues.T,
        skip_gain.reshape(1, C),
        out_weight,
    )
    return pl.pallas_call(
        turn_kernel,
        out_shape=jax.ShapeDtypeStruct((O, T), BF16),
        compiler_params=pltpu.CompilerParams(vmem_limit_bytes=60 * 1024 * 1024),
        name="turn",
    )(rows)


def solution(mesh):
    return jax.shard_map(
        on_device,
        mesh=mesh,
        in_specs=(
            P(None, "tp", "ctx"),
            P(None, "tp", "ctx"),
            P(None, "tp", None),
            P("tp", None),
            P("tp", None),
            P("tp"),
            P("tp", None),
        ),
        out_specs=P("tp", "ctx"),
        check_vma=False,
    )
```
